32 devices in a mesh: grp: 4 (over y, x), sp: 8 (over z, core).
Axes of the slice: x: 2, y: 2, z: 4, core: 2. Of those that a mesh axis runs over, the one named last changes fastest.
Arguments:
- coarse: bfloat16 [64, 48, 1024], P(('grp', 'sp')), parts along dimension 0, may hold values from -30 to 30
- conv_weight: bfloat16 [1024, 3, 3, 1024], P('sp'), may hold values from -0.104166667 to 0.104166667
- conv_bias: float32 [1024], P('sp'), may hold values from -5 to 5
- norm_gain: float32 [1024], P('sp'), may hold values from 0.5 to 1.5
- norm_shift: float32 [1024], P('sp'), may hold values from -3 to 3
- up_weight: bfloat16 [512, 2, 2, 1024], P('sp'), may hold values from -0.1875 to 0.1875
- up_bias: bfloat16 [512], P('sp'), may hold values from -3 to 3
Outputs:
- fine: bfloat16 [128, 96, 512], P(('grp', 'sp')), parts along dimension 0
The draws below stay inside these ranges and needn't reach their ends.
There are 4 independent parts, one for each index of `grp`. The reference program is written for one: setup_inputs(seed, part) draws one part's arguments, and reference() takes and returns one part's arrays. A program takes and returns all parts, laid end to end along the dimension named above; an argument that names none is the same for every part. Nothing has to cross between parts.
All inputs are finite; a program needn't handle non-finite values.
Results may differ from the reference program's by a relative error of at most 0.0042.
Values may be sent and summed in bfloat16 or wider, within the bound.
A program may use at most 64 MiB of HBM per device.

```python
import math
import jax
import jax.numpy as jnp
from jax import lax

CH = 1024
OUT = 512
GSIZE = 32
COLS = 48
HEIGHT = 16


def draw_coarse(key, part):
    first, second, third = jax.random.split(key, 3)
    pixel = jnp.exp(jax.random.uniform(second, (HEIGHT, COLS, 1), jnp.float32, math.log(0.3), math.log(3.0)))
    channel = jnp.exp(jax.random.uniform(third, (1, 1, CH), jnp.float32, math.log(0.5), math.log(2.0)))
    values = jax.random.normal(first, (HEIGHT, COLS, CH), jnp.float32)
    values = jnp.clip(values, -5.0, 5.0)
    return (values * pixel * channel).astype(jnp.bfloat16)


def draw_conv_weight(key, part):
    first, second = jax.random.split(key, 2)
    column = jnp.exp(jax.random.uniform(second, (CH, 1, 1, 1), jnp.float32, math.log(0.5), math.log(2.0)))
    values = jnp.clip(jax.random.normal(first, (CH, 3, 3, CH), jnp.float32), -5.0, 5.0)
    return (values * column * (9.0 * CH) ** (-0.5)).astype(jnp.bfloat16)


def levels(stream_key, shape, pieces, low, high):
    level = 1.0
    for axis_at, shards_of in pieces:
        steps = jax.random.uniform(jax.random.fold_in(jax.random.fold_in(stream_key, 6), axis_at), (shards_of,), jnp.float32, low / len(pieces), high / len(pieces))
        level = level * jnp.repeat(jnp.exp(steps), shape[axis_at] // shards_of).reshape((-1,) + (1,) * (len(shape) - 1 - axis_at))
    return level


def gaussian(stream_key, shape, deviation, bound, pieces=(), dtype=jnp.bfloat16):
    result = deviation * jax.random.normal(stream_key, shape, jnp.float32)
    if pieces:
        result = result * levels(stream_key, shape, pieces, -0.22, 0.18)
    return jnp.clip(result, -bound, bound).astype(dtype)


def setup_inputs(seed: int = 0, part: int = 0) -> dict:
    splits = jax.random.split(jax.random.key(seed), 8)
    part_splits = jax.random.split(jax.random.fold_in(splits[7], part), 8)
    return {
        "coarse": draw_coarse(jax.random.fold_in(jax.random.fold_in(splits[7], part), 71), part),
        "conv_weight": draw_conv_weight(jax.random.fold_in(splits[7], 71), part),
        "conv_bias": gaussian(splits[2], (CH,), 1.0, 5.0, ((0, 8),), jnp.float32),
        "norm_gain": jnp.clip(1.0 + 0.1 * jax.random.normal(splits[3], (CH,), jnp.float32), 0.5, 1.5),
        "norm_shift": gaussian(splits[4], (CH,), 0.5, 3.0, ((0, 8),), jnp.float32),
        "up_weight": gaussian(splits[5], (OUT, 2, 2, CH), CH ** -0.5, 0.1875, ((0, 8),)),
        "up_bias": gaussian(splits[6], (OUT,), 0.5, 3.0, ((0, 8),)),
    }


def reference(coarse, conv_weight, conv_bias, norm_gain, norm_shift, up_weight, up_bias):
    image = coarse.astype(jnp.float32)[None]
    kernel = jnp.transpose(conv_weight.astype(jnp.float32), (1, 2, 3, 0))
    convolved = lax.conv_general_dilated(image, kernel, (1, 1), 'SAME', dimension_numbers=('NHWC', 'HWIO', 'NHWC'), precision=lax.Precision.HIGHEST)[0]
    convolved = convolved + conv_bias
    grouped = convolved.reshape(HEIGHT, COLS, CH // GSIZE, GSIZE)
    centre = lax.optimization_barrier(jnp.mean(grouped, axis=(0, 1, 3), keepdims=True))
    spread = lax.optimization_barrier(jnp.mean(jnp.square(grouped - centre), axis=(0, 1, 3), keepdims=True))
    normed = ((grouped - centre) * lax.rsqrt(spread + 1e-05)).reshape(HEIGHT, COLS, CH)
    activated = jax.nn.silu(normed * norm_gain + norm_shift).astype(jnp.bfloat16)
    decoded = jnp.einsum('ijc,oabc->iajbo', activated.astype(jnp.float32), up_weight.astype(jnp.float32), precision=lax.Precision.HIGHEST)
    decoded = decoded.reshape(2 * HEIGHT, 2 * COLS, OUT) + up_bias
    return decoded.astype(jnp.bfloat16)
```

```python
import functools

import jax
import jax.numpy as jnp
from jax import lax
from jax.experimental import pallas as pl
from jax.experimental.pallas import tpu as pltpu
from jax.sharding import PartitionSpec as P

GSIZE = 32
TAPS = 4
NT = (((1,), (1,)), ((), ()))


def kernel(
    chips,
    coarse,
    conv_w,
    up_w,
    conv_bias,
    gain,
    shift,
    up_bias,
    out,
    gathered,
    w_vmem,
    up_all,
    summed,
    act,
    act_all,
    bias_own,
    bias_all,
    local_sem,
    c_line,
    c_sib,
    c_recv,
    u_line,
    u_xy,
    u_sib,
    u_recv,
    b_send,
    b_recv,
    a_send,
    a_recv,
):
    devices = 2 * chips
    rows, width, channels = coarse.shape
    outputs = conv_w.shape[0] // 9
    slice_out = up_w.shape[1]
    decoded = devices * slice_out
    me = lax.axis_index("sp")
    col = lax.axis_index("grp")
    z = me // 2
    core = me % 2
    sibling = 2 * z + 1 - core
    part = col % TAPS
    base = col - part

    def at(column, index):
        return {"grp": column, "sp": index}

    def remote(src, dst, send, recv, device):
        return pltpu.make_async_remote_copy(
            src_ref=src,
            dst_ref=dst,
            send_sem=send,
            recv_sem=recv,
            device_id=device,
            device_id_type=pl.DeviceIdType.MESH,
        )

    def onward(direction):
        return (z + 1, z + 1 < chips) if direction == 0 else (z - 1, z - 1 >= 0)

    def origin(direction, k):
        return (z - k, z - k >= 0) if direction == 0 else (z + k, z + k < chips)

    def coarse_line(direction, src, h, ref):
        b = 2 * src + core
        target = 2 * onward(direction)[0] + core
        return remote(ref, gathered.at[b, h], c_line.at[direction, src, h], c_recv.at[b, h], at(col, target))

    def coarse_sib(src, h, ref):
        b = 2 * src + core
        return remote(ref, gathered.at[b, h], c_sib.at[src, h], c_recv.at[b, h], at(col, sibling))

    def coarse_wait(b, h):
        remote(gathered.at[b, h], gathered.at[b, h], c_sib.at[0, h], c_recv.at[b, h], at(col, sibling)).wait_recv()

    def up_line(direction, src, ref):
        b = 2 * src + core
        target = 2 * onward(direction)[0] + core
        return remote(ref, up_all.at[part, b], u_line.at[direction, src], u_recv.at[b, part], at(col, target))

    def up_xy(q, src):
        b = 2 * src + core
        ref = up_all.at[part, b]
        return remote(ref, ref, u_xy.at[q - 1, src], u_recv.at[b, part], at(base + (part + q) % TAPS, me))

    def up_sib(src, tap, ref):
        b = 2 * src + core
        return remote(ref, up_all.at[tap, b], u_sib.at[src, tap], u_recv.at[b, tap], at(col, sibling))

    def up_wait(b, tap):
        ref = up_all.at[tap, b]
        remote(ref, ref, u_sib.at[0, tap], u_recv.at[b, tap], at(col, sibling)).wait_recv()

    w_copy = pltpu.make_async_copy(conv_w, w_vmem, local_sem.at[0])
    own_copy = pltpu.make_async_copy(coarse, gathered.at[me], local_sem.at[1])
    up_copies = [
        pltpu.make_async_copy(up_w.at[tap], up_all.at[tap, me], local_sem.at[2 + tap]) for tap in range(TAPS)
    ]
    w_copy.start()
    own_copy.start()
    for copy in up_copies:
        copy.start()

    barrier = pltpu.get_barrier_semaphore()

    def greet(i, carry):
        other = lax.rem(me + i, devices)
        pl.semaphore_signal(barrier, inc=1, device_id=at(col, other), device_id_type=pl.DeviceIdType.MESH)
        return carry

    lax.fori_loop(1, devices, greet, 0)
    for q in range(1, TAPS):
        pl.semaphore_signal(
            barrier, inc=1, device_id=at(base + (part + q) % TAPS, me), device_id_type=pl.DeviceIdType.MESH
        )
    pl.semaphore_wait(barrier, devices - 1 + TAPS - 1)

    for h in range(rows):
        for direction in range(2):

            @pl.when(onward(direction)[1])
            def _():
                coarse_line(direction, z, h, coarse.at[h]).start()

        coarse_sib(z, h, coarse.at[h]).start()
    for direction in range(2):

        @pl.when(onward(direction)[1])
        def _():
            up_line(direction, z, up_w.at[part]).start()

    for tap in range(TAPS):
        up_sib(z, tap, up_w.at[tap]).start()

    lanes = lax.broadcasted_iota(jnp.int32, (slice_out, decoded), 1)
    line = lax.broadcasted_iota(jnp.int32, (slice_out, decoded), 0)
    chosen = (lanes == line + me * slice_out).astype(jnp.float32)
    placed = jnp.dot(up_bias[...], chosen, preferred_element_type=jnp.float32, precision=lax.Precision.HIGHEST)
    bias_own[...] = placed
    bias_all[me] = placed

    def bias_copy(other, slot):
        return remote(bias_own, bias_all.at[slot], b_send.at[other], b_recv.at[slot], at(col, other))

    def send_bias(i, carry):
        bias_copy(lax.rem(me + i, devices), me).start()
        return carry

    lax.fori_loop(1, devices, send_bias, 0)

    summed[...] = jnp.zeros_like(summed)
    count = 2 * rows * width
    column = lax.broadcasted_iota(jnp.int32, (count, outputs), 0) % width

    def conv_pair(src):
        block = gathered[pl.ds(2 * src, 2)].reshape(count, channels)
        if outputs % 128 == 0:
            product = lax.dot_general(block, w_vmem[...], NT, preferred_element_type=jnp.float32)
            taps = [product[:, t * outputs : (t + 1) * outputs] for t in range(9)]
        else:
            taps = [
                lax.dot_general(
                    block, w_vmem[t * outputs : (t + 1) * outputs], NT, preferred_element_type=jnp.float32
                )
                for t in range(9)
            ]
        for r in range(3):
            left, middle, right = taps[3 * r : 3 * r + 3]
            total = (
                middle
                + jnp.where(column == 0, 0.0, pltpu.roll(left, 1, 0))
                + jnp.where(column == width - 1, 0.0, pltpu.roll(right, count - 1, 0))
            )
            where = pl.ds(2 * rows * src + 2 - r, 2 * rows)
            summed[where] = summed[where] + total.reshape(2 * rows, width, outputs)

    w_copy.wait()
    own_copy.wait()
    for h in range(rows):
        coarse_wait(sibling, h)
    conv_pair(z)

    def spread(k):
        for direction in range(2):
            src, there = origin(direction, k)

            @pl.when(there)
            def _():
                for q in range(1, TAPS):
                    tap = (part + q) % TAPS
                    up_wait(2 * src + core, tap)
                    up_sib(src, tap, up_all.at[tap, 2 * src + core]).start()

    def step(k, carry):
        for direction in range(2):
            src, there = origin(direction, k)

            @pl.when(there)
            def _():
                b = 2 * src + core
                for h in range(rows):
                    coarse_wait(b, h)

                    @pl.when(onward(direction)[1])
                    def _():
                        coarse_line(direction, src, h, gathered.at[b, h]).start()

                    coarse_sib(src, h, gathered.at[b, h]).start()

        for direction in range(2):
            src, there = origin(direction, k)

            @pl.when(there)
            def _():
                b = 2 * src + core
                up_wait(b, part)

                @pl.when(onward(direction)[1])
                def _():
                    up_line(direction, src, up_all.at[part, b]).start()

                for q in range(1, TAPS):
                    up_xy(q, src).start()
                up_sib(src, part, up_all.at[part, b]).start()

        for direction in range(2):
            src, there = origin(direction, k)

            @pl.when(there)
            def _():
                for h in range(rows):
                    coarse_wait(2 * src + 1 - core, h)
                conv_pair(src)

        @pl.when(k > 1)
        def _():
            spread(k - 1)

        return carry

    lax.fori_loop(1, chips, step, 0)

    height = devices * rows
    values = summed[1 : height + 1].reshape(height * width, outputs) + conv_bias[...]
    scale = 1.0 / (height * width * GSIZE)
    same = (
        lax.broadcasted_iota(jnp.int32, (outputs, outputs), 0) // GSIZE
        == lax.broadcasted_iota(jnp.int32, (outputs, outputs), 1) // GSIZE
    ).astype(jnp.float32)

    def group_mean(array):
        each = jnp.broadcast_to(jnp.sum(array, axis=0, keepdims=True), (8, outputs))
        whole = jnp.dot(each, same, preferred_element_type=jnp.float32, precision=lax.Precision.HIGHEST)
        return whole[:1] * scale

    values = values - group_mean(values)
    factor = lax.rsqrt(group_mean(values * values) + 1e-05) * gain[...]
    normed = values * factor + shift[...]
    act[...] = (normed / (1.0 + jnp.exp(-normed))).astype(jnp.bfloat16).reshape(devices, rows * width, outputs)

    def act_copy(other, slot):
        return remote(act.at[other], act_all.at[slot], a_send.at[other], a_recv.at[slot], at(col, other))

    def send_act(i, carry):
        act_copy(lax.rem(me + i, devices), me).start()
        return carry

    lax.fori_loop(1, devices, send_act, 0)
    act_all[me] = act[me]

    spread(chips - 1)

    def arrivals(i, carry):
        other = lax.rem(me + i, devices)
        bias_copy(other, other).wait_recv()
        act_copy(other, other).wait_recv()
        return carry

    lax.fori_loop(1, devices, arrivals, 0)

    def up_arrivals(src, carry):
        for tap in range(TAPS):
            up_wait(2 * src + 1 - core, tap)
        return carry

    lax.fori_loop(0, chips, up_arrivals, 0)
    for copy in up_copies:
        copy.wait()

    bias = jnp.sum(bias_all[...], axis=0)[:1]
    for tap in range(TAPS):
        weight = up_all[tap].reshape(decoded, channels)
        if outputs % 128 == 0:
            features = jnp.concatenate([act_all[s] for s in range(devices)], axis=1)
            fine = lax.dot_general(features, weight, NT, preferred_element_type=jnp.float32)
        else:
            fine = jnp.zeros((rows * width, decoded), jnp.float32)
            for s in range(devices):
                fine = fine + lax.dot_general(
                    act_all[s],
                    weight[:, s * outputs : (s + 1) * outputs],
                    NT,
                    preferred_element_type=jnp.float32,
                )
        a, b = tap // 2, tap % 2
        out[:, a, :, b * decoded : (b + 1) * decoded] = (
            (fine + bias).astype(jnp.bfloat16).reshape(rows, width, decoded)
        )

    def sent(src, carry):
        for h in range(rows):
            coarse_sib(src, h, gathered.at[0, h]).wait_send()
        for tap in range(TAPS):
            up_sib(src, tap, up_all.at[tap, 0]).wait_send()

        @pl.when(src != z)
        def _():
            for q in range(1, TAPS):
                up_xy(q, src).wait_send()

        for direction in range(2):
            passed = src <= z if direction == 0 else src >= z

            @pl.when(jnp.logical_and(passed, onward(direction)[1]))
            def _():
                for h in range(rows):
                    coarse_line(direction, src, h, gathered.at[0, h]).wait_send()
                up_line(direction, src, up_all.at[0, 0]).wait_send()

        return carry

    lax.fori_loop(0, chips, sent, 0)

    def small_sent(i, carry):
        other = lax.rem(me + i, devices)
        bias_copy(other, other).wait_send()
        act_copy(other, other).wait_send()
        return carry

    lax.fori_loop(1, devices, small_sent, 0)


def body(chips, coarse, conv_weight, conv_bias, norm_gain, norm_shift, up_weight, up_bias):
    devices = 2 * chips
    rows, width, channels = coarse.shape
    outputs = conv_weight.shape[0]
    slice_out = up_weight.shape[0]
    decoded = devices * slice_out
    conv_w = jnp.transpose(conv_weight, (1, 2, 0, 3)).reshape(9 * outputs, channels)
    up_w = jnp.transpose(up_weight, (1, 2, 0, 3)).reshape(TAPS, slice_out, channels)
    bias = jnp.broadcast_to(up_bias.astype(jnp.float32), (8, slice_out))
    anywhere = pl.BlockSpec(memory_space=pl.ANY)
    vmem = pl.BlockSpec(memory_space=pltpu.VMEM)
    dma = pltpu.SemaphoreType.DMA
    fine = pl.pallas_call(
        functools.partial(kernel, chips),
        out_shape=jax.ShapeDtypeStruct((rows, 2, width, 2 * decoded), jnp.bfloat16),
        in_specs=[anywhere] * 3 + [vmem] * 4,
        out_specs=vmem,
        scratch_shapes=[
            pltpu.VMEM((devices, rows, width, channels), jnp.bfloat16),
            pltpu.VMEM((9 * outputs, channels), jnp.bfloat16),
            pltpu.VMEM((TAPS, devices, slice_out, channels), jnp.bfloat16),
            pltpu.VMEM((devices * rows + 2, width, outputs), jnp.float32),
            pltpu.VMEM((devices, rows * width, outputs), jnp.bfloat16),
            pltpu.VMEM((devices, rows * width, outputs), jnp.bfloat16),
            pltpu.VMEM((8, decoded), jnp.float32),
            pltpu.VMEM((devices, 8, decoded), jnp.float32),
            dma((2 + TAPS,)),
            dma((2, chips, rows)),
            dma((chips, rows)),
            dma((devices, rows)),
            dma((2, chips)),
            dma((TAPS - 1, chips)),
            dma((chips, TAPS)),
            dma((devices, TAPS)),
            dma((devices,)),
            dma((devices,)),
            dma((devices,)),
            dma((devices,)),
        ],
        compiler_params=pltpu.CompilerParams(
            collective_id=0, has_side_effects=True, vmem_limit_bytes=48 * 1024 * 1024
        ),
    )(
        coarse,
        conv_w,
        up_w,
        conv_bias.reshape(1, outputs),
        norm_gain.reshape(1, outputs),
        norm_shift.reshape(1, outputs),
        bias,
    )
    return fine.reshape(2 * rows, 2 * width, decoded)


def solution(mesh):
    return jax.shard_map(
        functools.partial(body, mesh.shape["sp"] // 2),
        mesh=mesh,
        in_specs=(
            P(("grp", "sp"), None, None),
            P("sp", None, None, None),
            P("sp"),
            P("sp"),
            P("sp"),
            P("sp", None, None, None),
            P("sp"),
        ),
        out_specs=P(("grp", "sp"), None, None),
        check_vma=False,
    )
```

```python
import functools

import jax
import jax.numpy as jnp
from jax import lax
from jax.experimental import pallas as pl
from jax.experimental.pallas import tpu as pltpu
from jax.sharding import PartitionSpec as P

GSIZE = 32
TAPS = 4
NT = (((1,), (1,)), ((), ()))


def kernel(
    chips,
    coarse,
    conv_w,
    up_w,
    bias_hbm,
    gain_hbm,
    shift_hbm,
    up_bias,
    out,
    gathered,
    w_vmem,
    up_all,
    summed,
    act,
    act_all,
    bias_own,
    bias_all,
    conv_bias,
    gain,
    shift,
    local_sem,
    c_line,
    c_sib,
    c_recv,
    u_line,
    u_xy,
    u_sib,
    u_recv,
    b_send,
    b_recv,
    a_send,
    a_recv,
):
    devices = 2 * chips
    rows, width, channels = coarse.shape
    outputs = conv_w.shape[0] // 9
    slice_out = up_w.shape[1]
    decoded = devices * slice_out
    me = lax.axis_index("sp")
    col = lax.axis_index("grp")
    z = me // 2
    core = me % 2
    sibling = 2 * z + 1 - core
    part = col % TAPS
    base = col - part

    def at(column, index):
        return {"grp": column, "sp": index}

    def remote(src, dst, send, recv, device):
        return pltpu.make_async_remote_copy(
            src_ref=src,
            dst_ref=dst,
            send_sem=send,
            recv_sem=recv,
            device_id=device,
            device_id_type=pl.DeviceIdType.MESH,
        )

    def onward(direction):
        return (z + 1, z + 1 < chips) if direction == 0 else (z - 1, z - 1 >= 0)

    def origin(direction, k):
        return (z - k, z - k >= 0) if direction == 0 else (z + k, z + k < chips)

    def coarse_line(direction, src, h, ref):
        b = 2 * src + core
        target = 2 * onward(direction)[0] + core
        return remote(ref, gathered.at[b, h], c_line.at[direction, src, h], c_recv.at[b, h], at(col, target))

    def coarse_sib(src, h, ref):
        b = 2 * src + core
        return remote(ref, gathered.at[b, h], c_sib.at[src, h], c_recv.at[b, h], at(col, sibling))

    def coarse_wait(b, h):
        remote(gathered.at[b, h], gathered.at[b, h], c_sib.at[0, h], c_recv.at[b, h], at(col, sibling)).wait_recv()

    def up_direct(chip):
        target = 2 * chip + core
        return remote(up_w.at[part], up_all.at[part, me], u_line.at[chip], u_recv.at[me, part], at(col, target))

    def up_xy(q, src):
        b = 2 * src + core
        ref = up_all.at[part, b]
        return remote(ref, ref, u_xy.at[q - 1, src], u_recv.at[b, part], at(base + (part + q) % TAPS, me))

    def up_sib(src, tap, ref):
        b = 2 * src + core
        return remote(ref, up_all.at[tap, b], u_sib.at[src, tap], u_recv.at[b, tap], at(col, sibling))

    def up_wait(b, tap):
        ref = up_all.at[tap, b]
        remote(ref, ref, u_sib.at[0, tap], u_recv.at[b, tap], at(col, sibling)).wait_recv()

    w_copy = pltpu.make_async_copy(conv_w, w_vmem, local_sem.at[0])
    own_copy = pltpu.make_async_copy(coarse, gathered.at[me], local_sem.at[1])
    up_copies = [
        pltpu.make_async_copy(up_w.at[tap], up_all.at[tap, me], local_sem.at[2 + tap]) for tap in range(TAPS)
    ]
    small = [
        pltpu.make_async_copy(src, dst, local_sem.at[2 + TAPS + i])
        for i, (src, dst) in enumerate(((bias_hbm, conv_bias), (gain_hbm, gain), (shift_hbm, shift)))
    ]
    for copy in [own_copy, w_copy] + up_copies + small:
        copy.start()

    barrier = pltpu.get_barrier_semaphore()

    def greet(i, carry):
        other = lax.rem(me + i, devices)
        pl.semaphore_signal(barrier, inc=1, device_id=at(col, other), device_id_type=pl.DeviceIdType.MESH)
        return carry

    lax.fori_loop(1, devices, greet, 0)
    for q in range(1, TAPS):
        pl.semaphore_signal(
            barrier, inc=1, device_id=at(base + (part + q) % TAPS, me), device_id_type=pl.DeviceIdType.MESH
        )
    pl.semaphore_wait(barrier, devices - 1 + TAPS - 1)

    for h in range(rows):
        for direction in range(2):

            @pl.when(onward(direction)[1])
            def _():
                coarse_line(direction, z, h, coarse.at[h]).start()

        coarse_sib(z, h, coarse.at[h]).start()

    def send_up(k, carry):
        for direction in range(2):
            chip, there = origin(direction, k)

            @pl.when(there)
            def _():
                up_direct(chip).start()

        return carry

    lax.fori_loop(1, chips, send_up, 0)
    for tap in range(TAPS):
        up_sib(z, tap, up_w.at[tap]).start()

    lanes = lax.broadcasted_iota(jnp.int32, (slice_out, decoded), 1)
    line = lax.broadcasted_iota(jnp.int32, (slice_out, decoded), 0)
    chosen = (lanes == line + me * slice_out).astype(jnp.float32)
    placed = jnp.dot(up_bias[...], chosen, preferred_element_type=jnp.float32, precision=lax.Precision.HIGHEST)
    bias_own[...] = placed
    bias_all[me] = placed

    def bias_copy(other, slot):
        return remote(bias_own, bias_all.at[slot], b_send.at[other], b_recv.at[slot], at(col, other))

    def send_bias(i, carry):
        bias_copy(lax.rem(me + i, devices), me).start()
        return carry

    lax.fori_loop(1, devices, send_bias, 0)

    summed[...] = jnp.zeros_like(summed)
    count = 2 * rows * width
    column = lax.broadcasted_iota(jnp.int32, (count, outputs), 0) % width

    def conv_pair(src):
        block = gathered[pl.ds(2 * src, 2)].reshape(count, channels)
        if outputs % 128 == 0:
            product = lax.dot_general(block, w_vmem[...], NT, preferred_element_type=jnp.float32)
            taps = [product[:, t * outputs : (t + 1) * outputs] for t in range(9)]
        else:
            taps = [
                lax.dot_general(
                    block, w_vmem[t * outputs : (t + 1) * outputs], NT, preferred_element_type=jnp.float32
                )
                for t in range(9)
            ]
        for r in range(3):
            left, middle, right = taps[3 * r : 3 * r + 3]
            total = (
                middle
                + jnp.where(column == 0, 0.0, pltpu.roll(left, 1, 0))
                + jnp.where(column == width - 1, 0.0, pltpu.roll(right, count - 1, 0))
            )
            where = pl.ds(2 * rows * src + 2 - r, 2 * rows)
            summed[where] = summed[where] + total.reshape(2 * rows, width, outputs)

    w_copy.wait()
    own_copy.wait()
    for h in range(rows):
        coarse_wait(sibling, h)
    conv_pair(z)

    def spread(k):
        for direction in range(2):
            src, there = origin(direction, k)

            @pl.when(there)
            def _():
                for q in range(1, TAPS):
                    tap = (part + q) % TAPS
                    up_wait(2 * src + core, tap)
                    up_sib(src, tap, up_all.at[tap, 2 * src + core]).start()

    def step(k, carry):
        for direction in range(2):
            src, there = origin(direction, k)

            @pl.when(there)
            def _():
                b = 2 * src + core
                for h in range(rows):
                    coarse_wait(b, h)

                    @pl.when(onward(direction)[1])
                    def _():
                        coarse_line(direction, src, h, gathered.at[b, h]).start()

                    coarse_sib(src, h, gathered.at[b, h]).start()

        for direction in range(2):
            src, there = origin(direction, k)

            @pl.when(there)
            def _():
                b = 2 * src + core
                up_wait(b, part)
                for q in range(1, TAPS):
                    up_xy(q, src).start()
                up_sib(src, part, up_all.at[part, b]).start()

        for direction in range(2):
            src, there = origin(direction, k)

            @pl.when(there)
            def _():
                for h in range(rows):
                    coarse_wait(2 * src + 1 - core, h)
                conv_pair(src)

        @pl.when(k > 1)
        def _():
            spread(k - 1)

        return carry

    lax.fori_loop(1, chips, step, 0)

    height = devices * rows
    for copy in small:
        copy.wait()
    values = summed[1 : height + 1].reshape(height * width, outputs) + conv_bias[...]
    scale = 1.0 / (height * width * GSIZE)
    same = (
        lax.broadcasted_iota(jnp.int32, (outputs, outputs), 0) // GSIZE
        == lax.broadcasted_iota(jnp.int32, (outputs, outputs), 1) // GSIZE
    ).astype(jnp.float32)

    def group_mean(array):
        each = jnp.broadcast_to(jnp.sum(array, axis=0, keepdims=True), (8, outputs))
        whole = jnp.dot(each, same, preferred_element_type=jnp.float32, precision=lax.Precision.HIGHEST)
        return whole[:1] * scale

    values = values - group_mean(values)
    factor = lax.rsqrt(group_mean(values * values) + 1e-05) * gain[...]
    normed = values * factor + shift[...]
    act[...] = (normed / (1.0 + jnp.exp(-normed))).astype(jnp.bfloat16).reshape(devices, rows * width, outputs)

    def act_copy(other, slot):
        return remote(act.at[other], act_all.at[slot], a_send.at[other], a_recv.at[slot], at(col, other))

    def send_act(i, carry):
        act_copy(lax.rem(me + i, devices), me).start()
        return carry

    lax.fori_loop(1, devices, send_act, 0)
    act_all[me] = act[me]

    spread(chips - 1)

    def arrivals(i, carry):
        other = lax.rem(me + i, devices)
        bias_copy(other, other).wait_recv()
        act_copy(other, other).wait_recv()
        return carry

    lax.fori_loop(1, devices, arrivals, 0)

    def up_arrivals(src, carry):
        for tap in range(TAPS):
            up_wait(2 * src + 1 - core, tap)
        return carry

    lax.fori_loop(0, chips, up_arrivals, 0)
    for copy in up_copies:
        copy.wait()

    bias = jnp.sum(bias_all[...], axis=0)[:1]
    for tap in range(TAPS):
        weight = up_all[tap].reshape(decoded, channels)
        if outputs % 128 == 0:
            features = jnp.concatenate([act_all[s] for s in range(devices)], axis=1)
            fine = lax.dot_general(features, weight, NT, preferred_element_type=jnp.float32)
        else:
            fine = jnp.zeros((rows * width, decoded), jnp.float32)
            for s in range(devices):
                fine = fine + lax.dot_general(
                    act_all[s],
                    weight[:, s * outputs : (s + 1) * outputs],
                    NT,
                    preferred_element_type=jnp.float32,
                )
        a, b = tap // 2, tap % 2
        out[:, a, :, b * decoded : (b + 1) * decoded] = (
            (fine + bias).astype(jnp.bfloat16).reshape(rows, width, decoded)
        )

    def sent(src, carry):
        for h in range(rows):
            coarse_sib(src, h, gathered.at[0, h]).wait_send()
        for tap in range(TAPS):
            up_sib(src, tap, up_all.at[tap, 0]).wait_send()

        @pl.when(src != z)
        def _():
            up_direct(src).wait_send()
            for q in range(1, TAPS):
                up_xy(q, src).wait_send()

        for direction in range(2):
            passed = src <= z if direction == 0 else src >= z

            @pl.when(jnp.logical_and(passed, onward(direction)[1]))
            def _():
                for h in range(rows):
                    coarse_line(direction, src, h, gathered.at[0, h]).wait_send()

        return carry

    lax.fori_loop(0, chips, sent, 0)

    def small_sent(i, carry):
        other = lax.rem(me + i, devices)
        bias_copy(other, other).wait_send()
        act_copy(other, other).wait_send()
        return carry

    lax.fori_loop(1, devices, small_sent, 0)


def body(chips, coarse, conv_weight, conv_bias, norm_gain, norm_shift, up_weight, up_bias):
    devices = 2 * chips
    rows, width, channels = coarse.shape
    outputs = conv_weight.shape[0]
    slice_out = up_weight.shape[0]
    decoded = devices * slice_out
    conv_w = jnp.transpose(conv_weight, (1, 2, 0, 3)).reshape(9 * outputs, channels)
    up_w = jnp.transpose(up_weight, (1, 2, 0, 3)).reshape(TAPS, slice_out, channels)
    bias = jnp.broadcast_to(up_bias.astype(jnp.float32), (8, slice_out))
    hbm = pl.BlockSpec(memory_space=pltpu.HBM)
    vmem = pl.BlockSpec(memory_space=pltpu.VMEM)
    dma = pltpu.SemaphoreType.DMA
    fine = pl.pallas_call(
        functools.partial(kernel, chips),
        out_shape=jax.ShapeDtypeStruct((rows, 2, width, 2 * decoded), jnp.bfloat16),
        in_specs=[hbm] * 6 + [vmem],
        out_specs=vmem,
        scratch_shapes=[
            pltpu.VMEM((devices, rows, width, channels), jnp.bfloat16),
            pltpu.VMEM((9 * outputs, channels), jnp.bfloat16),
            pltpu.VMEM((TAPS, devices, slice_out, channels), jnp.bfloat16),
            pltpu.VMEM((devices * rows + 2, width, outputs), jnp.float32),
            pltpu.VMEM((devices, rows * width, outputs), jnp.bfloat16),
            pltpu.VMEM((devices, rows * width, outputs), jnp.bfloat16),
            pltpu.VMEM((8, decoded), jnp.float32),
            pltpu.VMEM((devices, 8, decoded), jnp.float32),
            pltpu.VMEM((1, outputs), jnp.float32),
            pltpu.VMEM((1, outputs), jnp.float32),
            pltpu.VMEM((1, outputs), jnp.float32),
            dma((5 + TAPS,)),
            dma((2, chips, rows)),
            dma((chips, rows)),
            dma((devices, rows)),
            dma((chips,)),
            dma((TAPS - 1, chips)),
            dma((chips, TAPS)),
            dma((devices, TAPS)),
            dma((devices,)),
            dma((devices,)),
            dma((devices,)),
            dma((devices,)),
        ],
        compiler_params=pltpu.CompilerParams(
            collective_id=0, has_side_effects=True, vmem_limit_bytes=60 * 1024 * 1024
        ),
    )(
        coarse,
        conv_w,
        up_w,
        conv_bias.reshape(1, outputs),
        norm_gain.reshape(1, outputs),
        norm_shift.reshape(1, outputs),
        bias,
    )
    return fine.reshape(2 * rows, 2 * width, decoded)


def solution(mesh):
    return jax.shard_map(
        functools.partial(body, mesh.shape["sp"] // 2),
        mesh=mesh,
        in_specs=(
            P(("grp", "sp"), None, None),
            P("sp", None, None, None),
            P("sp"),
            P("sp"),
            P("sp"),
            P("sp", None, None, None),
            P("sp"),
        ),
        out_specs=P(("grp", "sp"), None, None),
        check_vma=False,
    )
```

```python
import functools

import jax
import jax.numpy as jnp
from jax import lax
from jax.experimental import pallas as pl
from jax.experimental.pallas import tpu as pltpu
from jax.sharding import PartitionSpec as P

GSIZE = 32
TAPS = 4
NT = (((1,), (1,)), ((), ()))


def kernel(
    chips,
    coarse,
    conv_w,
    up_w,
    bias_hbm,
    gain_hbm,
    shift_hbm,
    up_bias,
    out,
    gathered,
    w_vmem,
    up_all,
    summed,
    act,
    act_all,
    bias_own,
    bias_all,
    conv_bias,
    gain,
    shift,
    mixed,
    bias_raw,
    local_sem,
    c_line,
    c_sib,
    c_recv,
    u_line,
    u_xy,
    u_sib,
    u_recv,
    b_send,
    b_recv,
    a_send,
    a_recv,
):
    devices = 2 * chips
    rows, width, channels = coarse.shape
    outputs = conv_w.shape[0] // 9
    slice_out = up_w.shape[1]
    decoded = devices * slice_out
    me = lax.axis_index("sp")
    col = lax.axis_index("grp")
    z = me // 2
    core = me % 2
    sibling = 2 * z + 1 - core
    part = col % TAPS
    base = col - part

    def at(column, index):
        return {"grp": column, "sp": index}

    def remote(src, dst, send, recv, device):
        return pltpu.make_async_remote_copy(
            src_ref=src,
            dst_ref=dst,
            send_sem=send,
            recv_sem=recv,
            device_id=device,
            device_id_type=pl.DeviceIdType.MESH,
        )

    def onward(direction):
        return (z + 1, z + 1 < chips) if direction == 0 else (z - 1, z - 1 >= 0)

    def origin(direction, k):
        return (z - k, z - k >= 0) if direction == 0 else (z + k, z + k < chips)

    def coarse_line(direction, src, h, ref):
        b = 2 * src + core
        target = 2 * onward(direction)[0] + core
        return remote(ref, gathered.at[b, h], c_line.at[direction, src, h], c_recv.at[b, h], at(col, target))

    def coarse_sib(src, h, ref):
        b = 2 * src + core
        return remote(ref, gathered.at[b, h], c_sib.at[src, h], c_recv.at[b, h], at(col, sibling))

    def coarse_wait(b, h):
        remote(gathered.at[b, h], gathered.at[b, h], c_sib.at[0, h], c_recv.at[b, h], at(col, sibling)).wait_recv()

    def up_line(direction, src, ref):
        b = 2 * src + core
        target = 2 * onward(direction)[0] + core
        return remote(ref, up_all.at[part, b], u_line.at[direction, src], u_recv.at[b, part], at(col, target))

    def up_xy(q, src):
        b = 2 * src + core
        ref = up_all.at[part, b]
        return remote(ref, ref, u_xy.at[q - 1, src], u_recv.at[b, part], at(base + (part + q) % TAPS, me))

    def up_sib(src, tap, ref):
        b = 2 * src + core
        return remote(ref, up_all.at[tap, b], u_sib.at[src, tap], u_recv.at[b, tap], at(col, sibling))

    def up_wait(b, tap):
        ref = up_all.at[tap, b]
        remote(ref, ref, u_sib.at[0, tap], u_recv.at[b, tap], at(col, sibling)).wait_recv()

    w_copy = pltpu.make_async_copy(conv_w, w_vmem, local_sem.at[0])
    own_copy = pltpu.make_async_copy(coarse, gathered.at[me], local_sem.at[1])
    up_copies = [
        pltpu.make_async_copy(up_w.at[tap], up_all.at[tap, me], local_sem.at[2 + tap]) for tap in range(TAPS)
    ]
    small = [
        pltpu.make_async_copy(src, dst, local_sem.at[2 + TAPS + i])
        for i, (src, dst) in enumerate(((bias_hbm, conv_bias), (gain_hbm, gain), (shift_hbm, shift)))
    ]
    bias_copy_in = pltpu.make_async_copy(up_bias, bias_raw, local_sem.at[5 + TAPS])
    for copy in [own_copy, w_copy, bias_copy_in] + up_copies + small:
        copy.start()

    barrier = pltpu.get_barrier_semaphore()

    def greet(i, carry):
        other = lax.rem(me + i, devices)
        pl.semaphore_signal(barrier, inc=1, device_id=at(col, other), device_id_type=pl.DeviceIdType.MESH)
        return carry

    lax.fori_loop(1, devices, greet, 0)
    for q in range(1, TAPS):
        pl.semaphore_signal(
            barrier, inc=1, device_id=at(base + (part + q) % TAPS, me), device_id_type=pl.DeviceIdType.MESH
        )
    pl.semaphore_wait(barrier, devices - 1 + TAPS - 1)

    for h in range(rows):
        for direction in range(2):

            @pl.when(onward(direction)[1])
            def _():
                coarse_line(direction, z, h, coarse.at[h]).start()

        coarse_sib(z, h, coarse.at[h]).start()
    for tap in range(TAPS):
        up_sib(z, tap, up_w.at[tap]).start()

    lanes = lax.broadcasted_iota(jnp.int32, (slice_out, decoded), 1)
    line = lax.broadcasted_iota(jnp.int32, (slice_out, decoded), 0)
    chosen = (lanes == line + me * slice_out).astype(jnp.float32)
    bias_copy_in.wait()
    raw = jnp.broadcast_to(bias_raw[...].astype(jnp.float32).reshape(1, slice_out), (8, slice_out))
    placed = jnp.dot(raw, chosen, preferred_element_type=jnp.float32, precision=lax.Precision.HIGHEST)
    bias_own[...] = placed
    bias_all[me] = placed

    def bias_copy(other, slot):
        return remote(bias_own, bias_all.at[slot], b_send.at[other], b_recv.at[slot], at(col, other))

    def send_bias(i, carry):
        bias_copy(lax.rem(me + i, devices), me).start()
        return carry

    lax.fori_loop(1, devices, send_bias, 0)

    summed[...] = jnp.zeros_like(summed)
    count = 2 * rows * width
    column = lax.broadcasted_iota(jnp.int32, (count, outputs), 0) % width

    def conv_pair(src):
        block = gathered[pl.ds(2 * src, 2)].reshape(count, channels)
        if outputs % 128 == 0:
            product = lax.dot_general(block, w_vmem[...], NT, preferred_element_type=jnp.float32)
            taps = [product[:, t * outputs : (t + 1) * outputs] for t in range(9)]
        else:
            taps = [
                lax.dot_general(
                    block, w_vmem[t * outputs : (t + 1) * outputs], NT, preferred_element_type=jnp.float32
                )
                for t in range(9)
            ]
        for r in range(3):
            left, middle, right = taps[3 * r : 3 * r + 3]
            total = (
                middle
                + jnp.where(column == 0, 0.0, pltpu.roll(left, 1, 0))
                + jnp.where(column == width - 1, 0.0, pltpu.roll(right, count - 1, 0))
            )
            where = pl.ds(2 * rows * src + 2 - r, 2 * rows)
            summed[where] = summed[where] + total.reshape(2 * rows, width, outputs)

    w_copy.wait()
    own_copy.wait()
    for h in range(rows):
        coarse_wait(sibling, h)
    conv_pair(z)

    for direction in range(2):

        @pl.when(onward(direction)[1])
        def _():
            for h in range(rows):
                coarse_line(direction, z, h, coarse.at[h]).wait_send()
            up_line(direction, z, up_w.at[part]).start()

    def spread(k):
        for direction in range(2):
            src, there = origin(direction, k)

            @pl.when(there)
            def _():
                for q in range(1, TAPS):
                    tap = (part + q) % TAPS
                    up_wait(2 * src + core, tap)
                    up_sib(src, tap, up_all.at[tap, 2 * src + core]).start()

    def pass_up(k):
        for direction in range(2):
            src, there = origin(direction, k)

            @pl.when(there)
            def _():
                b = 2 * src + core
                up_wait(b, part)

                @pl.when(onward(direction)[1])
                def _():
                    up_line(direction, src, up_all.at[part, b]).start()

                for q in range(1, TAPS):
                    up_xy(q, src).start()
                up_sib(src, part, up_all.at[part, b]).start()

    def step(k, carry):
        for direction in range(2):
            src, there = origin(direction, k)

            @pl.when(there)
            def _():
                b = 2 * src + core
                for h in range(rows):
                    coarse_wait(b, h)

                    @pl.when(onward(direction)[1])
                    def _():
                        coarse_line(direction, src, h, gathered.at[b, h]).start()

                    coarse_sib(src, h, gathered.at[b, h]).start()

        @pl.when(k > 1)
        def _():
            pass_up(k - 1)

        for direction in range(2):
            src, there = origin(direction, k)

            @pl.when(there)
            def _():
                for h in range(rows):
                    coarse_wait(2 * src + 1 - core, h)
                conv_pair(src)

        @pl.when(k > 2)
        def _():
            spread(k - 2)

        return carry

    lax.fori_loop(1, chips, step, 0)

    height = devices * rows
    for copy in small:
        copy.wait()
    values = summed[1 : height + 1].reshape(height * width, outputs) + conv_bias[...]
    scale = 1.0 / (height * width * GSIZE)
    same = (
        lax.broadcasted_iota(jnp.int32, (outputs, outputs), 0) // GSIZE
        == lax.broadcasted_iota(jnp.int32, (outputs, outputs), 1) // GSIZE
    ).astype(jnp.float32)

    def group_mean(array):
        each = jnp.broadcast_to(jnp.sum(array, axis=0, keepdims=True), (8, outputs))
        whole = jnp.dot(each, same, preferred_element_type=jnp.float32, precision=lax.Precision.HIGHEST)
        return whole[:1] * scale

    values = values - group_mean(values)
    factor = lax.rsqrt(group_mean(values * values) + 1e-05) * gain[...]
    normed = values * factor + shift[...]
    act[...] = (normed / (1.0 + jnp.exp(-normed))).astype(jnp.bfloat16).reshape(devices, rows * width, outputs)

    def act_copy(other, slot):
        return remote(act.at[other], act_all.at[slot], a_send.at[other], a_recv.at[slot], at(col, other))

    def send_act(i, carry):
        act_copy(lax.rem(me + i, devices), me).start()
        return carry

    lax.fori_loop(1, devices, send_act, 0)
    act_all[me] = act[me]

    pass_up(chips - 1)
    if chips > 2:
        spread(chips - 2)
    spread(chips - 1)

    def arrivals(i, carry):
        other = lax.rem(me + i, devices)
        bias_copy(other, other).wait_recv()
        act_copy(other, other).wait_recv()
        return carry

    lax.fori_loop(1, devices, arrivals, 0)

    def up_arrivals(src, carry):
        for tap in range(TAPS):
            up_wait(2 * src + 1 - core, tap)
        return carry

    lax.fori_loop(0, chips, up_arrivals, 0)
    for copy in up_copies:
        copy.wait()

    bias = jnp.sum(bias_all[...], axis=0)[:1]
    for tap in range(TAPS):
        weight = up_all[tap].reshape(decoded, channels)
        if outputs % 128 == 0:
            features = jnp.concatenate([act_all[s] for s in range(devices)], axis=1)
            fine = lax.dot_general(features, weight, NT, preferred_element_type=jnp.float32)
        else:
            fine = jnp.zeros((rows * width, decoded), jnp.float32)
            for s in range(devices):
                fine = fine + lax.dot_general(
                    act_all[s],
                    weight[:, s * outputs : (s + 1) * outputs],
                    NT,
                    preferred_element_type=jnp.float32,
                )
        a, b = tap // 2, tap % 2
        for i in range(rows):
            values = fine[i * width : (i + 1) * width] + bias
            for t in range(decoded // 128):
                mixed[t, 2 * i + a, pl.ds(b, width, stride=2), :] = values[:, 128 * t : 128 * (t + 1)]
    for t in range(decoded // 128):
        out[:, :, 128 * t : 128 * (t + 1)] = mixed[t].astype(jnp.bfloat16)

    def sent(src, carry):
        for h in range(rows):
            coarse_sib(src, h, gathered.at[0, h]).wait_send()
        for tap in range(TAPS):
            up_sib(src, tap, up_all.at[tap, 0]).wait_send()

        @pl.when(src != z)
        def _():
            for q in range(1, TAPS):
                up_xy(q, src).wait_send()

        for direction in range(2):
            passed = src <= z if direction == 0 else src >= z

            @pl.when(jnp.logical_and(passed, onward(direction)[1]))
            def _():
                @pl.when(src != z)
                def _():
                    for h in range(rows):
                        coarse_line(direction, src, h, gathered.at[0, h]).wait_send()

                up_line(direction, src, up_all.at[0, 0]).wait_send()

        return carry

    lax.fori_loop(0, chips, sent, 0)

    def small_sent(i, carry):
        other = lax.rem(me + i, devices)
        bias_copy(other, other).wait_send()
        act_copy(other, other).wait_send()
        return carry

    lax.fori_loop(1, devices, small_sent, 0)


def body(chips, coarse, conv_weight, conv_bias, norm_gain, norm_shift, up_weight, up_bias):
    devices = 2 * chips
    rows, width, channels = coarse.shape
    outputs = conv_weight.shape[0]
    slice_out = up_weight.shape[0]
    decoded = devices * slice_out
    conv_w = jnp.transpose(conv_weight, (1, 2, 0, 3)).reshape(9 * outputs, channels)
    up_w = jnp.transpose(up_weight, (1, 2, 0, 3)).reshape(TAPS, slice_out, channels)
    hbm = pl.BlockSpec(memory_space=pltpu.HBM)
    vmem = pl.BlockSpec(memory_space=pltpu.VMEM)
    dma = pltpu.SemaphoreType.DMA
    return pl.pallas_call(
        functools.partial(kernel, chips),
        out_shape=jax.ShapeDtypeStruct((2 * rows, 2 * width, decoded), jnp.bfloat16),
        in_specs=[hbm, hbm, pl.BlockSpec(memory_space=pl.ANY), hbm, hbm, hbm, hbm],
        out_specs=vmem,
        scratch_shapes=[
            pltpu.VMEM((devices, rows, width, channels), jnp.bfloat16),
            pltpu.VMEM((9 * outputs, channels), jnp.bfloat16),
            pltpu.VMEM((TAPS, devices, slice_out, channels), jnp.bfloat16),
            pltpu.VMEM((devices * rows + 2, width, outputs), jnp.float32),
            pltpu.VMEM((devices, rows * width, outputs), jnp.bfloat16),
            pltpu.VMEM((devices, rows * width, outputs), jnp.bfloat16),
            pltpu.VMEM((8, decoded), jnp.float32),
            pltpu.VMEM((devices, 8, decoded), jnp.float32),
            pltpu.VMEM((1, outputs), jnp.float32),
            pltpu.VMEM((1, outputs), jnp.float32),
            pltpu.VMEM((1, outputs), jnp.float32),
            pltpu.VMEM((decoded // 128, 2 * rows, 2 * width, 128), jnp.float32),
            pltpu.VMEM((slice_out,), jnp.bfloat16),
            dma((6 + TAPS,)),
            dma((2, chips, rows)),
            dma((chips, rows)),
            dma((devices, rows)),
            dma((2, chips)),
            dma((TAPS - 1, chips)),
            dma((chips, TAPS)),
            dma((devices, TAPS)),
            dma((devices,)),
            dma((devices,)),
            dma((devices,)),
            dma((devices,)),
        ],
        compiler_params=pltpu.CompilerParams(
            collective_id=0, has_side_effects=True, vmem_limit_bytes=60 * 1024 * 1024
        ),
    )(
        coarse,
        conv_w,
        up_w,
        conv_bias.reshape(1, outputs),
        norm_gain.reshape(1, outputs),
        norm_shift.reshape(1, outputs),
        up_bias,
    )


def solution(mesh):
    return jax.shard_map(
        functools.partial(body, mesh.shape["sp"] // 2),
        mesh=mesh,
        in_specs=(
            P(("grp", "sp"), None, None),
            P("sp", None, None, None),
            P("sp"),
            P("sp"),
            P("sp"),
            P("sp", None, None, None),
            P("sp"),
        ),
        out_specs=P(("grp", "sp"), None, None),
        check_vma=False,
    )
```

```python
import functools

import jax
import jax.numpy as jnp
from jax import lax
from jax.experimental import pallas as pl
from jax.experimental.pallas import tpu as pltpu
from jax.sharding import PartitionSpec as P

GSIZE = 32
TAPS = 4
NT = (((1,), (1,)), ((), ()))


def kernel(
    chips,
    coarse,
    conv_w,
    up_w,
    bias_hbm,
    gain_hbm,
    shift_hbm,
    up_bias,
    out,
    gathered,
    w_vmem,
    up_all,
    summed,
    act,
    act_all,
    bias_own,
    bias_all,
    conv_bias,
    gain,
    shift,
    mixed,
    bias_raw,
    local_sem,
    c_line,
    c_sib,
    c_recv,
    u_line,
    u_xy,
    u_sib,
    u_recv,
    u_whole,
    b_send,
    b_recv,
    a_send,
    a_recv,
):
    devices = 2 * chips
    rows, width, channels = coarse.shape
    outputs = conv_w.shape[0] // 9
    slice_out = up_w.shape[1]
    decoded = devices * slice_out
    me = lax.axis_index("sp")
    col = lax.axis_index("grp")
    z = me // 2
    core = me % 2
    sibling = 2 * z + 1 - core
    part = col % TAPS
    base = col - part

    def at(column, index):
        return {"grp": column, "sp": index}

    def remote(src, dst, send, recv, device):
        return pltpu.make_async_remote_copy(
            src_ref=src,
            dst_ref=dst,
            send_sem=send,
            recv_sem=recv,
            device_id=device,
            device_id_type=pl.DeviceIdType.MESH,
        )

    def onward(direction):
        return (z + 1, z + 1 < chips) if direction == 0 else (z - 1, z - 1 >= 0)

    def origin(direction, k):
        return (z - k, z - k >= 0) if direction == 0 else (z + k, z + k < chips)

    def coarse_line(direction, src, h, ref):
        b = 2 * src + core
        target = 2 * onward(direction)[0] + core
        return remote(ref, gathered.at[b, h], c_line.at[direction, src, h], c_recv.at[b, h], at(col, target))

    def coarse_sib(src, h, ref):
        b = 2 * src + core
        return remote(ref, gathered.at[b, h], c_sib.at[src, h], c_recv.at[b, h], at(col, sibling))

    def coarse_wait(b, h):
        remote(gathered.at[b, h], gathered.at[b, h], c_sib.at[0, h], c_recv.at[b, h], at(col, sibling)).wait_recv()

    def up_line(direction, src, ref):
        b = 2 * src + core
        target = 2 * onward(direction)[0] + core
        return remote(ref, up_all.at[part, b], u_line.at[direction, src], u_recv.at[b, part], at(col, target))

    def up_xy(q, src):
        b = 2 * src + core
        ref = up_all.at[part, b]
        return remote(ref, ref, u_xy.at[q - 1, src], u_recv.at[b, part], at(base + (part + q) % TAPS, me))

    def up_sib(src, ref):
        b = 2 * src + core
        return remote(ref, up_all.at[:, b], u_sib.at[src], u_whole.at[b], at(col, sibling))

    def up_wait(b, tap):
        ref = up_all.at[tap, b]
        remote(ref, ref, u_xy.at[0, 0], u_recv.at[b, tap], at(col, sibling)).wait_recv()

    w_copy = pltpu.make_async_copy(conv_w, w_vmem, local_sem.at[0])
    own_copy = pltpu.make_async_copy(coarse, gathered.at[me], local_sem.at[1])
    up_copies = [
        pltpu.make_async_copy(up_w.at[tap], up_all.at[tap, me], local_sem.at[2 + tap]) for tap in range(TAPS)
    ]
    small = [
        pltpu.make_async_copy(src, dst, local_sem.at[2 + TAPS + i])
        for i, (src, dst) in enumerate(((bias_hbm, conv_bias), (gain_hbm, gain), (shift_hbm, shift)))
    ]
    bias_copy_in = pltpu.make_async_copy(up_bias, bias_raw, local_sem.at[5 + TAPS])
    for copy in [own_copy, w_copy, bias_copy_in] + up_copies + small:
        copy.start()

    barrier = pltpu.get_barrier_semaphore()

    def greet(i, carry):
        other = lax.rem(me + i, devices)
        pl.semaphore_signal(barrier, inc=1, device_id=at(col, other), device_id_type=pl.DeviceIdType.MESH)
        return carry

    lax.fori_loop(1, devices, greet, 0)
    for q in range(1, TAPS):
        pl.semaphore_signal(
            barrier, inc=1, device_id=at(base + (part + q) % TAPS, me), device_id_type=pl.DeviceIdType.MESH
        )
    pl.semaphore_wait(barrier, devices - 1 + TAPS - 1)

    for h in range(rows):
        for direction in range(2):

            @pl.when(onward(direction)[1])
            def _():
                coarse_line(direction, z, h, coarse.at[h]).start()

        coarse_sib(z, h, coarse.at[h]).start()
    for direction in range(2):

        @pl.when(onward(direction)[1])
        def _():
            up_line(direction, z, up_w.at[part]).start()

    up_sib(z, up_w).start()

    lanes = lax.broadcasted_iota(jnp.int32, (slice_out, decoded), 1)
    line = lax.broadcasted_iota(jnp.int32, (slice_out, decoded), 0)
    chosen = (lanes == line + me * slice_out).astype(jnp.float32)
    bias_copy_in.wait()
    raw = jnp.broadcast_to(bias_raw[...].astype(jnp.float32).reshape(1, slice_out), (8, slice_out))
    placed = jnp.dot(raw, chosen, preferred_element_type=jnp.float32, precision=lax.Precision.HIGHEST)
    bias_own[...] = placed
    bias_all[me] = placed

    def bias_copy(other, slot):
        return remote(bias_own, bias_all.at[slot], b_send.at[other], b_recv.at[slot], at(col, other))

    def send_bias(i, carry):
        bias_copy(lax.rem(me + i, devices), me).start()
        return carry

    lax.fori_loop(1, devices, send_bias, 0)

    summed[...] = jnp.zeros_like(summed)
    count = 2 * rows * width
    column = lax.broadcasted_iota(jnp.int32, (count, outputs), 0) % width

    def conv_pair(src):
        block = gathered[pl.ds(2 * src, 2)].reshape(count, channels)
        if outputs % 128 == 0:
            product = lax.dot_general(block, w_vmem[...], NT, preferred_element_type=jnp.float32)
            taps = [product[:, t * outputs : (t + 1) * outputs] for t in range(9)]
        else:
            taps = [
                lax.dot_general(
                    block, w_vmem[t * outputs : (t + 1) * outputs], NT, preferred_element_type=jnp.float32
                )
                for t in range(9)
            ]
        for r in range(3):
            left, middle, right = taps[3 * r : 3 * r + 3]
            total = (
                middle
                + jnp.where(column == 0, 0.0, pltpu.roll(left, 1, 0))
                + jnp.where(column == width - 1, 0.0, pltpu.roll(right, count - 1, 0))
            )
            where = pl.ds(2 * rows * src + 2 - r, 2 * rows)
            summed[where] = summed[where] + total.reshape(2 * rows, width, outputs)

    w_copy.wait()
    own_copy.wait()
    for h in range(rows):
        coarse_wait(sibling, h)
    conv_pair(z)

    def spread(k):
        for direction in range(2):
            src, there = origin(direction, k)

            @pl.when(there)
            def _():
                for q in range(1, TAPS):
                    tap = (part + q) % TAPS
                    up_wait(2 * src + core, tap)
                up_sib(src, up_all.at[:, 2 * src + core]).start()

    def pass_up(k):
        for direction in range(2):
            src, there = origin(direction, k)

            @pl.when(there)
            def _():
                b = 2 * src + core
                up_wait(b, part)

                @pl.when(onward(direction)[1])
                def _():
                    up_line(direction, src, up_all.at[part, b]).start()

                for q in range(1, TAPS):
                    up_xy(q, src).start()

    def step(k, carry):
        for direction in range(2):
            src, there = origin(direction, k)

            @pl.when(there)
            def _():
                b = 2 * src + core
                for h in range(rows):
                    coarse_wait(b, h)

                    @pl.when(onward(direction)[1])
                    def _():
                        coarse_line(direction, src, h, gathered.at[b, h]).start()

                    coarse_sib(src, h, gathered.at[b, h]).start()

        pass_up(k)

        for direction in range(2):
            src, there = origin(direction, k)

            @pl.when(there)
            def _():
                for h in range(rows):
                    coarse_wait(2 * src + 1 - core, h)
                conv_pair(src)

        @pl.when(k > 1)
        def _():
            spread(k - 1)

        return carry

    lax.fori_loop(1, chips, step, 0)

    height = devices * rows
    for copy in small:
        copy.wait()
    values = summed[1 : height + 1].reshape(height * width, outputs) + conv_bias[...]
    scale = 1.0 / (height * width * GSIZE)
    same = (
        lax.broadcasted_iota(jnp.int32, (outputs, outputs), 0) // GSIZE
        == lax.broadcasted_iota(jnp.int32, (outputs, outputs), 1) // GSIZE
    ).astype(jnp.float32)

    def group_mean(array):
        each = jnp.broadcast_to(jnp.sum(array, axis=0, keepdims=True), (8, outputs))
        whole = jnp.dot(each, same, preferred_element_type=jnp.float32, precision=lax.Precision.HIGHEST)
        return whole[:1] * scale

    values = values - group_mean(values)
    factor = lax.rsqrt(group_mean(values * values) + 1e-05) * gain[...]
    normed = values * factor + shift[...]
    act[...] = (normed / (1.0 + jnp.exp(-normed))).astype(jnp.bfloat16).reshape(devices, rows * width, outputs)

    def act_copy(other, slot):
        return remote(act.at[other], act_all.at[slot], a_send.at[other], a_recv.at[slot], at(col, other))

    def send_act(i, carry):
        act_copy(lax.rem(me + i, devices), me).start()
        return carry

    lax.fori_loop(1, devices, send_act, 0)
    act_all[me] = act[me]

    def early(i, carry):
        other = lax.rem(me + i, devices)
        bias_copy(other, other).wait()
        return carry

    lax.fori_loop(1, devices, early, 0)

    def coarse_sent(src, carry):
        for h in range(rows):
            coarse_sib(src, h, gathered.at[0, h]).wait_send()
        for direction in range(2):
            passed = src <= z if direction == 0 else src >= z

            @pl.when(jnp.logical_and(passed, onward(direction)[1]))
            def _():
                for h in range(rows):
                    coarse_line(direction, src, h, gathered.at[0, h]).wait_send()
                up_line(direction, src, up_all.at[0, 0]).wait_send()

        return carry

    lax.fori_loop(0, chips, coarse_sent, 0)
    spread(chips - 1)
    for copy in up_copies:
        copy.wait()

    def arrivals(i, carry):
        other = lax.rem(me + i, devices)
        act_copy(other, other).wait()
        return carry

    lax.fori_loop(1, devices, arrivals, 0)

    def up_arrivals(src, carry):
        @pl.when(src != z)
        def _():
            for q in range(1, TAPS):
                up_xy(q, src).wait_send()

        up_sib(src, up_all.at[:, 0]).wait_send()
        b = 2 * src + 1 - core
        remote(up_all.at[:, b], up_all.at[:, b], u_sib.at[src], u_whole.at[b], at(col, sibling)).wait_recv()
        return carry

    lax.fori_loop(0, chips, up_arrivals, 0)

    bias = jnp.sum(bias_all[...], axis=0)[:1]
    for tap in range(TAPS):
        weight = up_all[tap].reshape(decoded, channels)
        if outputs % 128 == 0:
            features = jnp.concatenate([act_all[s] for s in range(devices)], axis=1)
            fine = lax.dot_general(features, weight, NT, preferred_element_type=jnp.float32)
        else:
            fine = jnp.zeros((rows * width, decoded), jnp.float32)
            for s in range(devices):
                fine = fine + lax.dot_general(
                    act_all[s],
                    weight[:, s * outputs : (s + 1) * outputs],
                    NT,
                    preferred_element_type=jnp.float32,
                )
        a, b = tap // 2, tap % 2
        for i in range(rows):
            values = fine[i * width : (i + 1) * width] + bias
            for t in range(decoded // 128):
                mixed[t, 2 * i + a, pl.ds(b, width, stride=2), :] = values[:, 128 * t : 128 * (t + 1)]
    for t in range(decoded // 128):
        out[:, :, 128 * t : 128 * (t + 1)] = mixed[t].astype(jnp.bfloat16)


def body(chips, coarse, conv_weight, conv_bias, norm_gain, norm_shift, up_weight, up_bias):
    devices = 2 * chips
    rows, width, channels = coarse.shape
    outputs = conv_weight.shape[0]
    slice_out = up_weight.shape[0]
    decoded = devices * slice_out
    conv_w = jnp.transpose(conv_weight, (1, 2, 0, 3)).reshape(9 * outputs, channels)
    up_w = jnp.transpose(up_weight, (1, 2, 0, 3)).reshape(TAPS, slice_out, channels)
    hbm = pl.BlockSpec(memory_space=pltpu.HBM)
    vmem = pl.BlockSpec(memory_space=pltpu.VMEM)
    dma = pltpu.SemaphoreType.DMA
    return pl.pallas_call(
        functools.partial(kernel, chips),
        out_shape=jax.ShapeDtypeStruct((2 * rows, 2 * width, decoded), jnp.bfloat16),
        in_specs=[hbm, hbm, pl.BlockSpec(memory_space=pl.ANY), hbm, hbm, hbm, hbm],
        out_specs=vmem,
        scratch_shapes=[
            pltpu.VMEM((devices, rows, width, channels), jnp.bfloat16),
            pltpu.VMEM((9 * outputs, channels), jnp.bfloat16),
            pltpu.VMEM((TAPS, devices, slice_out, channels), jnp.bfloat16),
            pltpu.VMEM((devices * rows + 2, width, outputs), jnp.float32),
            pltpu.VMEM((devices, rows * width, outputs), jnp.bfloat16),
            pltpu.VMEM((devices, rows * width, outputs), jnp.bfloat16),
            pltpu.VMEM((8, decoded), jnp.float32),
            pltpu.VMEM((devices, 8, decoded), jnp.float32),
            pltpu.VMEM((1, outputs), jnp.float32),
            pltpu.VMEM((1, outputs), jnp.float32),
            pltpu.VMEM((1, outputs), jnp.float32),
            pltpu.VMEM((decoded // 128, 2 * rows, 2 * width, 128), jnp.float32),
            pltpu.VMEM((slice_out,), jnp.bfloat16),
            dma((6 + TAPS,)),
            dma((2, chips, rows)),
            dma((chips, rows)),
            dma((devices, rows)),
            dma((2, chips)),
            dma((TAPS - 1, chips)),
            dma((chips,)),
            dma((devices, TAPS)),
            dma((devices,)),
            dma((devices,)),
            dma((devices,)),
            dma((devices,)),
            dma((devices,)),
        ],
        compiler_params=pltpu.CompilerParams(
            collective_id=0, has_side_effects=True, vmem_limit_bytes=60 * 1024 * 1024
        ),
    )(
        coarse,
        conv_w,
        up_w,
        conv_bias.reshape(1, outputs),
        norm_gain.reshape(1, outputs),
        norm_shift.reshape(1, outputs),
        up_bias,
    )


def solution(mesh):
    return jax.shard_map(
        functools.partial(body, mesh.shape["sp"] // 2),
        mesh=mesh,
        in_specs=(
            P(("grp", "sp"), None, None),
            P("sp", None, None, None),
            P("sp"),
            P("sp"),
            P("sp"),
            P("sp", None, None, None),
            P("sp"),
        ),
        out_specs=P(("grp", "sp"), None, None),
        check_vma=False,
    )
```

```python
import functools

import jax
import jax.numpy as jnp
from jax import lax
from jax.experimental import pallas as pl
from jax.experimental.pallas import tpu as pltpu
from jax.sharding import PartitionSpec as P

GSIZE = 32
TAPS = 4
NT = (((1,), (1,)), ((), ()))


def kernel(
    chips,
    coarse,
    conv_w,
    up_w,
    bias_hbm,
    gain_hbm,
    shift_hbm,
    up_bias,
    out,
    gathered,
    w_vmem,
    up_all,
    summed,
    act,
    act_all,
    bias_own,
    bias_all,
    conv_bias,
    gain,
    shift,
    mixed,
    bias_raw,
    local_sem,
    c_line,
    c_sib,
    c_recv,
    u_line,
    u_xy,
    u_sib,
    u_recv,
    u_whole,
    b_send,
    b_recv,
    a_send,
    a_recv,
):
    devices = 2 * chips
    rows, width, channels = coarse.shape
    outputs = conv_w.shape[0] // 9
    slice_out = up_w.shape[1]
    decoded = devices * slice_out
    me = lax.axis_index("sp")
    col = lax.axis_index("grp")
    z = me // 2
    core = me % 2
    sibling = 2 * z + 1 - core
    part = col % TAPS
    base = col - part

    def at(column, index):
        return {"grp": column, "sp": index}

    def remote(src, dst, send, recv, device):
        return pltpu.make_async_remote_copy(
            src_ref=src,
            dst_ref=dst,
            send_sem=send,
            recv_sem=recv,
            device_id=device,
            device_id_type=pl.DeviceIdType.MESH,
        )

    def onward(direction):
        return (z + 1, z + 1 < chips) if direction == 0 else (z - 1, z - 1 >= 0)

    def origin(direction, k):
        return (z - k, z - k >= 0) if direction == 0 else (z + k, z + k < chips)

    def coarse_line(direction, src, h, ref):
        b = 2 * src + core
        target = 2 * onward(direction)[0] + core
        return remote(ref, gathered.at[b, h], c_line.at[direction, src, h], c_recv.at[b, h], at(col, target))

    def coarse_sib(src, h, ref):
        b = 2 * src + core
        return remote(ref, gathered.at[b, h], c_sib.at[src, h], c_recv.at[b, h], at(col, sibling))

    def coarse_wait(b, h):
        remote(gathered.at[b, h], gathered.at[b, h], c_sib.at[0, h], c_recv.at[b, h], at(col, sibling)).wait_recv()

    def up_line(direction, src, ref):
        b = 2 * src + core
        target = 2 * onward(direction)[0] + core
        return remote(ref, up_all.at[part, b], u_line.at[direction, src], u_recv.at[b, part], at(col, target))

    def up_xy(q, src):
        b = 2 * src + core
        ref = up_all.at[part, b]
        return remote(ref, ref, u_xy.at[q - 1, src], u_recv.at[b, part], at(base + (part + q) % TAPS, me))

    def up_sib(src, ref):
        b = 2 * src + core
        return remote(ref, up_all.at[:, b], u_sib.at[src], u_whole.at[b], at(col, sibling))

    def up_wait(b, tap):
        ref = up_all.at[tap, b]
        remote(ref, ref, u_xy.at[0, 0], u_recv.at[b, tap], at(col, sibling)).wait_recv()

    w_copy = pltpu.make_async_copy(conv_w, w_vmem, local_sem.at[0])
    own_copy = pltpu.make_async_copy(coarse, gathered.at[me], local_sem.at[1])
    up_copies = [
        pltpu.make_async_copy(up_w.at[tap], up_all.at[tap, me], local_sem.at[2 + tap]) for tap in range(TAPS)
    ]
    small = [
        pltpu.make_async_copy(src, dst, local_sem.at[2 + TAPS + i])
        for i, (src, dst) in enumerate(((bias_hbm, conv_bias), (gain_hbm, gain), (shift_hbm, shift)))
    ]
    bias_copy_in = pltpu.make_async_copy(up_bias, bias_raw, local_sem.at[5 + TAPS])
    for copy in [own_copy, w_copy, bias_copy_in] + up_copies + small:
        copy.start()

    barrier = pltpu.get_barrier_semaphore()

    def greet(i, carry):
        other = lax.rem(me + i, devices)
        pl.semaphore_signal(barrier, inc=1, device_id=at(col, other), device_id_type=pl.DeviceIdType.MESH)
        return carry

    lax.fori_loop(1, devices, greet, 0)
    for q in range(1, TAPS):
        pl.semaphore_signal(
            barrier, inc=1, device_id=at(base + (part + q) % TAPS, me), device_id_type=pl.DeviceIdType.MESH
        )
    pl.semaphore_wait(barrier, devices - 1 + TAPS - 1)

    for h in range(rows):
        for direction in range(2):

            @pl.when(onward(direction)[1])
            def _():
                coarse_line(direction, z, h, coarse.at[h]).start()

        coarse_sib(z, h, coarse.at[h]).start()
    for direction in range(2):

        @pl.when(onward(direction)[1])
        def _():
            up_line(direction, z, up_w.at[part]).start()

    up_sib(z, up_w).start()

    lanes = lax.broadcasted_iota(jnp.int32, (slice_out, decoded), 1)
    line = lax.broadcasted_iota(jnp.int32, (slice_out, decoded), 0)
    chosen = (lanes == line + me * slice_out).astype(jnp.float32)
    bias_copy_in.wait()
    raw = jnp.broadcast_to(bias_raw[...].astype(jnp.float32).reshape(1, slice_out), (8, slice_out))
    placed = jnp.dot(raw, chosen, preferred_element_type=jnp.float32, precision=lax.Precision.HIGHEST)
    bias_own[...] = placed
    bias_all[me] = placed

    def bias_copy(other, slot):
        return remote(bias_own, bias_all.at[slot], b_send.at[other], b_recv.at[slot], at(col, other))

    def send_bias(i, carry):
        bias_copy(lax.rem(me + i, devices), me).start()
        return carry

    lax.fori_loop(1, devices, send_bias, 0)

    summed[...] = jnp.zeros_like(summed)
    count = 2 * rows * width
    column = lax.broadcasted_iota(jnp.int32, (count, outputs), 0) % width

    def conv_pair(src):
        block = gathered[pl.ds(2 * src, 2)].reshape(count, channels)
        if outputs % 128 == 0:
            product = lax.dot_general(block, w_vmem[...], NT, preferred_element_type=jnp.float32)
            taps = [product[:, t * outputs : (t + 1) * outputs] for t in range(9)]
        else:
            taps = [
                lax.dot_general(
                    block, w_vmem[t * outputs : (t + 1) * outputs], NT, preferred_element_type=jnp.float32
                )
                for t in range(9)
            ]
        for r in range(3):
            left, middle, right = taps[3 * r : 3 * r + 3]
            total = (
                middle
                + jnp.where(column == 0, 0.0, pltpu.roll(left, 1, 0))
                + jnp.where(column == width - 1, 0.0, pltpu.roll(right, count - 1, 0))
            )
            where = pl.ds(2 * rows * src + 2 - r, 2 * rows)
            summed[where] = summed[where] + total.reshape(2 * rows, width, outputs)

    w_copy.wait()
    own_copy.wait()
    for h in range(rows):
        coarse_wait(sibling, h)
    conv_pair(z)

    def spread(k):
        for direction in range(2):
            src, there = origin(direction, k)

            @pl.when(there)
            def _():
                for q in range(1, TAPS):
                    tap = (part + q) % TAPS
                    up_wait(2 * src + core, tap)
                up_sib(src, up_all.at[:, 2 * src + core]).start()

    def pass_up(k):
        for direction in range(2):
            src, there = origin(direction, k)

            @pl.when(there)
            def _():
                b = 2 * src + core
                up_wait(b, part)

                @pl.when(onward(direction)[1])
                def _():
                    up_line(direction, src, up_all.at[part, b]).start()

                for q in range(1, TAPS):
                    up_xy(q, src).start()

    def step(k, carry):
        for direction in range(2):
            src, there = origin(direction, k)

            @pl.when(there)
            def _():
                b = 2 * src + core
                for h in range(rows):
                    coarse_wait(b, h)

                    @pl.when(onward(direction)[1])
                    def _():
                        coarse_line(direction, src, h, gathered.at[b, h]).start()

                    coarse_sib(src, h, gathered.at[b, h]).start()

        @pl.when(k < chips - 1)
        def _():
            pass_up(k)

        for direction in range(2):
            src, there = origin(direction, k)

            @pl.when(there)
            def _():
                for h in range(rows):
                    coarse_wait(2 * src + 1 - core, h)
                conv_pair(src)

        @pl.when(k == chips - 1)
        def _():
            pass_up(k)

        @pl.when(jnp.logical_and(k > 1, k < chips - 1))
        def _():
            spread(k - 1)

        return carry

    lax.fori_loop(1, chips, step, 0)

    height = devices * rows
    for copy in small:
        copy.wait()
    values = summed[1 : height + 1].reshape(height * width, outputs) + conv_bias[...]
    scale = 1.0 / (height * width * GSIZE)
    same = (
        lax.broadcasted_iota(jnp.int32, (outputs, outputs), 0) // GSIZE
        == lax.broadcasted_iota(jnp.int32, (outputs, outputs), 1) // GSIZE
    ).astype(jnp.float32)

    def group_mean(array):
        each = jnp.broadcast_to(jnp.sum(array, axis=0, keepdims=True), (8, outputs))
        whole = jnp.dot(each, same, preferred_element_type=jnp.float32, precision=lax.Precision.HIGHEST)
        return whole[:1] * scale

    values = values - group_mean(values)
    factor = lax.rsqrt(group_mean(values * values) + 1e-05) * gain[...]
    normed = values * factor + shift[...]
    act[...] = (normed / (1.0 + jnp.exp(-normed))).astype(jnp.bfloat16).reshape(devices, rows * width, outputs)

    def act_copy(other, slot):
        return remote(act.at[other], act_all.at[slot], a_send.at[other], a_recv.at[slot], at(col, other))

    def send_act(i, carry):
        act_copy(lax.rem(me + i, devices), me).start()
        return carry

    lax.fori_loop(1, devices, send_act, 0)
    act_all[me] = act[me]

    if chips > 2:
        spread(chips - 2)

    def early(i, carry):
        other = lax.rem(me + i, devices)
        bias_copy(other, other).wait()
        return carry

    lax.fori_loop(1, devices, early, 0)

    def coarse_sent(src, carry):
        for h in range(rows):
            coarse_sib(src, h, gathered.at[0, h]).wait_send()
        for direction in range(2):
            passed = src <= z if direction == 0 else src >= z

            @pl.when(jnp.logical_and(passed, onward(direction)[1]))
            def _():
                for h in range(rows):
                    coarse_line(direction, src, h, gathered.at[0, h]).wait_send()
                up_line(direction, src, up_all.at[0, 0]).wait_send()

        return carry

    lax.fori_loop(0, chips, coarse_sent, 0)
    spread(chips - 1)
    for copy in up_copies:
        copy.wait()

    def arrivals(i, carry):
        other = lax.rem(me + i, devices)
        act_copy(other, other).wait()
        return carry

    lax.fori_loop(1, devices, arrivals, 0)

    def up_arrivals(src, carry):
        @pl.when(src != z)
        def _():
            for q in range(1, TAPS):
                up_xy(q, src).wait_send()

        up_sib(src, up_all.at[:, 0]).wait_send()
        b = 2 * src + 1 - core
        remote(up_all.at[:, b], up_all.at[:, b], u_sib.at[src], u_whole.at[b], at(col, sibling)).wait_recv()
        return carry

    lax.fori_loop(0, chips, up_arrivals, 0)

    bias = jnp.sum(bias_all[...], axis=0)[:1]
    for tap in range(TAPS):
        weight = up_all[tap].reshape(decoded, channels)
        if outputs % 128 == 0:
            features = jnp.concatenate([act_all[s] for s in range(devices)], axis=1)
            fine = lax.dot_general(features, weight, NT, preferred_element_type=jnp.float32)
        else:
            fine = jnp.zeros((rows * width, decoded), jnp.float32)
            for s in range(devices):
                fine = fine + lax.dot_general(
                    act_all[s],
                    weight[:, s * outputs : (s + 1) * outputs],
                    NT,
                    preferred_element_type=jnp.float32,
                )
        a, b = tap // 2, tap % 2
        for i in range(rows):
            values = fine[i * width : (i + 1) * width] + bias
            for t in range(decoded // 128):
                mixed[t, 2 * i + a, pl.ds(b, width, stride=2), :] = values[:, 128 * t : 128 * (t + 1)]
    for t in range(decoded // 128):
        out[:, :, 128 * t : 128 * (t + 1)] = mixed[t].astype(jnp.bfloat16)


def body(chips, coarse, conv_weight, conv_bias, norm_gain, norm_shift, up_weight, up_bias):
    devices = 2 * chips
    rows, width, channels = coarse.shape
    outputs = conv_weight.shape[0]
    slice_out = up_weight.shape[0]
    decoded = devices * slice_out
    conv_w = jnp.transpose(conv_weight, (1, 2, 0, 3)).reshape(9 * outputs, channels)
    up_w = jnp.transpose(up_weight, (1, 2, 0, 3)).reshape(TAPS, slice_out, channels)
    hbm = pl.BlockSpec(memory_space=pltpu.HBM)
    vmem = pl.BlockSpec(memory_space=pltpu.VMEM)
    dma = pltpu.SemaphoreType.DMA
    return pl.pallas_call(
        functools.partial(kernel, chips),
        out_shape=jax.ShapeDtypeStruct((2 * rows, 2 * width, decoded), jnp.bfloat16),
        in_specs=[hbm, hbm, pl.BlockSpec(memory_space=pl.ANY), hbm, hbm, hbm, hbm],
        out_specs=vmem,
        scratch_shapes=[
            pltpu.VMEM((devices, rows, width, channels), jnp.bfloat16),
            pltpu.VMEM((9 * outputs, channels), jnp.bfloat16),
            pltpu.VMEM((TAPS, devices, slice_out, channels), jnp.bfloat16),
            pltpu.VMEM((devices * rows + 2, width, outputs), jnp.float32),
            pltpu.VMEM((devices, rows * width, outputs), jnp.bfloat16),
            pltpu.VMEM((devices, rows * width, outputs), jnp.bfloat16),
            pltpu.VMEM((8, decoded), jnp.float32),
            pltpu.VMEM((devices, 8, decoded), jnp.float32),
            pltpu.VMEM((1, outputs), jnp.float32),
            pltpu.VMEM((1, outputs), jnp.float32),
            pltpu.VMEM((1, outputs), jnp.float32),
            pltpu.VMEM((decoded // 128, 2 * rows, 2 * width, 128), jnp.float32),
            pltpu.VMEM((slice_out,), jnp.bfloat16),
            dma((6 + TAPS,)),
            dma((2, chips, rows)),
            dma((chips, rows)),
            dma((devices, rows)),
            dma((2, chips)),
            dma((TAPS - 1, chips)),
            dma((chips,)),
            dma((devices, TAPS)),
            dma((devices,)),
            dma((devices,)),
            dma((devices,)),
            dma((devices,)),
            dma((devices,)),
        ],
        compiler_params=pltpu.CompilerParams(
            collective_id=0, has_side_effects=True, vmem_limit_bytes=60 * 1024 * 1024
        ),
    )(
        coarse,
        conv_w,
        up_w,
        conv_bias.reshape(1, outputs),
        norm_gain.reshape(1, outputs),
        norm_shift.reshape(1, outputs),
        up_bias,
    )


def solution(mesh):
    return jax.shard_map(
        functools.partial(body, mesh.shape["sp"] // 2),
        mesh=mesh,
        in_specs=(
            P(("grp", "sp"), None, None),
            P("sp", None, None, None),
            P("sp"),
            P("sp"),
            P("sp"),
            P("sp", None, None, None),
            P("sp"),
        ),
        out_specs=P(("grp", "sp"), None, None),
        check_vma=False,
    )
```

```python
import functools

import jax
import jax.numpy as jnp
from jax import lax
from jax.experimental import pallas as pl
from jax.experimental.pallas import tpu as pltpu
from jax.sharding import PartitionSpec as P

GSIZE = 32
TAPS = 4
NT = (((1,), (1,)), ((), ()))


def kernel(
    chips,
    coarse,
    conv_w,
    up_w,
    bias_hbm,
    gain_hbm,
    shift_hbm,
    up_bias,
    out,
    gathered,
    w_vmem,
    up_all,
    summed,
    act,
    act_all,
    bias_own,
    bias_all,
    conv_bias,
    gain,
    shift,
    mixed,
    bias_raw,
    local_sem,
    c_line,
    c_sib,
    c_recv,
    u_line,
    u_xy,
    u_sib,
    u_recv,
    u_whole,
    b_send,
    b_recv,
    a_send,
    a_recv,
):
    devices = 2 * chips
    rows, width, channels = coarse.shape
    outputs = conv_w.shape[0] // 9
    slice_out = up_w.shape[1]
    decoded = devices * slice_out
    me = lax.axis_index("sp")
    col = lax.axis_index("grp")
    z = me // 2
    core = me % 2
    sibling = 2 * z + 1 - core
    part = col % TAPS
    base = col - part

    def at(column, index):
        return {"grp": column, "sp": index}

    def remote(src, dst, send, recv, device):
        return pltpu.make_async_remote_copy(
            src_ref=src,
            dst_ref=dst,
            send_sem=send,
            recv_sem=recv,
            device_id=device,
            device_id_type=pl.DeviceIdType.MESH,
        )

    def onward(direction):
        return (z + 1, z + 1 < chips) if direction == 0 else (z - 1, z - 1 >= 0)

    def origin(direction, k):
        return (z - k, z - k >= 0) if direction == 0 else (z + k, z + k < chips)

    def coarse_line(direction, src, h, ref):
        b = 2 * src + core
        target = 2 * onward(direction)[0] + core
        return remote(ref, gathered.at[b, h], c_line.at[direction, src, h], c_recv.at[b, h], at(col, target))

    def coarse_sib(src, h, ref):
        b = 2 * src + core
        return remote(ref, gathered.at[b, h], c_sib.at[src, h], c_recv.at[b, h], at(col, sibling))

    def coarse_wait(b, h):
        remote(gathered.at[b, h], gathered.at[b, h], c_sib.at[0, h], c_recv.at[b, h], at(col, sibling)).wait_recv()

    def up_line(direction, src, ref):
        b = 2 * src + core
        target = 2 * onward(direction)[0] + core
        return remote(ref, up_all.at[part, b], u_line.at[direction, src], u_recv.at[b, part], at(col, target))

    def up_xy(q, src):
        b = 2 * src + core
        ref = up_all.at[part, b]
        return remote(ref, ref, u_xy.at[q - 1, src], u_recv.at[b, part], at(base + (part + q) % TAPS, me))

    def up_sib(src, ref):
        b = 2 * src + core
        return remote(ref, up_all.at[:, b], u_sib.at[src], u_whole.at[b], at(col, sibling))

    def up_wait(b, tap):
        ref = up_all.at[tap, b]
        remote(ref, ref, u_xy.at[0, 0], u_recv.at[b, tap], at(col, sibling)).wait_recv()

    w_copy = pltpu.make_async_copy(conv_w, w_vmem, local_sem.at[0])
    own_copy = pltpu.make_async_copy(coarse, gathered.at[me], local_sem.at[1])
    up_copies = [
        pltpu.make_async_copy(up_w.at[tap], up_all.at[tap, me], local_sem.at[2 + tap]) for tap in range(TAPS)
    ]
    small = [
        pltpu.make_async_copy(src, dst, local_sem.at[2 + TAPS + i])
        for i, (src, dst) in enumerate(((bias_hbm, conv_bias), (gain_hbm, gain), (shift_hbm, shift)))
    ]
    bias_copy_in = pltpu.make_async_copy(up_bias, bias_raw, local_sem.at[5 + TAPS])
    for copy in [own_copy, w_copy, bias_copy_in] + up_copies + small:
        copy.start()

    barrier = pltpu.get_barrier_semaphore()

    def greet(i, carry):
        other = lax.rem(me + i, devices)
        pl.semaphore_signal(barrier, inc=1, device_id=at(col, other), device_id_type=pl.DeviceIdType.MESH)
        return carry

    lax.fori_loop(1, devices, greet, 0)
    for q in range(1, TAPS):
        pl.semaphore_signal(
            barrier, inc=1, device_id=at(base + (part + q) % TAPS, me), device_id_type=pl.DeviceIdType.MESH
        )
    pl.semaphore_wait(barrier, devices - 1 + TAPS - 1)

    for direction in range(2):

        @pl.when(onward(direction)[1])
        def _():
            up_line(direction, z, up_w.at[part]).start()

    for h in range(rows):
        for direction in range(2):

            @pl.when(onward(direction)[1])
            def _():
                coarse_line(direction, z, h, coarse.at[h]).start()

        coarse_sib(z, h, coarse.at[h]).start()
    up_sib(z, up_w).start()

    lanes = lax.broadcasted_iota(jnp.int32, (slice_out, decoded), 1)
    line = lax.broadcasted_iota(jnp.int32, (slice_out, decoded), 0)
    chosen = (lanes == line + me * slice_out).astype(jnp.float32)
    bias_copy_in.wait()
    raw = jnp.broadcast_to(bias_raw[...].astype(jnp.float32).reshape(1, slice_out), (8, slice_out))
    placed = jnp.dot(raw, chosen, preferred_element_type=jnp.float32, precision=lax.Precision.HIGHEST)
    bias_own[...] = placed
    bias_all[me] = placed

    def bias_copy(other, slot):
        return remote(bias_own, bias_all.at[slot], b_send.at[other], b_recv.at[slot], at(col, other))

    def send_bias(i, carry):
        bias_copy(lax.rem(me + i, devices), me).start()
        return carry

    lax.fori_loop(1, devices, send_bias, 0)

    summed[...] = jnp.zeros_like(summed)
    count = 2 * rows * width
    column = lax.broadcasted_iota(jnp.int32, (count, outputs), 0) % width

    def conv_pair(src):
        block = gathered[pl.ds(2 * src, 2)].reshape(count, channels)
        if outputs % 128 == 0:
            product = lax.dot_general(block, w_vmem[...], NT, preferred_element_type=jnp.float32)
            taps = [product[:, t * outputs : (t + 1) * outputs] for t in range(9)]
        else:
            taps = [
                lax.dot_general(
                    block, w_vmem[t * outputs : (t + 1) * outputs], NT, preferred_element_type=jnp.float32
                )
                for t in range(9)
            ]
        for r in range(3):
            left, middle, right = taps[3 * r : 3 * r + 3]
            total = (
                middle
                + jnp.where(column == 0, 0.0, pltpu.roll(left, 1, 0))
                + jnp.where(column == width - 1, 0.0, pltpu.roll(right, count - 1, 0))
            )
            where = pl.ds(2 * rows * src + 2 - r, 2 * rows)
            summed[where] = summed[where] + total.reshape(2 * rows, width, outputs)

    w_copy.wait()
    own_copy.wait()
    for h in range(rows):
        coarse_wait(sibling, h)
    conv_pair(z)

    def spread(k):
        for direction in range(2):
            src, there = origin(direction, k)

            @pl.when(there)
            def _():
                for q in range(1, TAPS):
                    tap = (part + q) % TAPS
                    up_wait(2 * src + core, tap)
                up_sib(src, up_all.at[:, 2 * src + core]).start()

    def pass_up(k):
        for direction in range(2):
            src, there = origin(direction, k)

            @pl.when(there)
            def _():
                b = 2 * src + core
                up_wait(b, part)

                @pl.when(onward(direction)[1])
                def _():
                    up_line(direction, src, up_all.at[part, b]).start()

                for q in range(1, TAPS):
                    up_xy(q, src).start()

    def step(k, carry):
        for direction in range(2):
            src, there = origin(direction, k)

            @pl.when(there)
            def _():
                b = 2 * src + core
                for h in range(rows):
                    coarse_wait(b, h)

                    @pl.when(onward(direction)[1])
                    def _():
                        coarse_line(direction, src, h, gathered.at[b, h]).start()

                    coarse_sib(src, h, gathered.at[b, h]).start()

        pass_up(k)

        for direction in range(2):
            src, there = origin(direction, k)

            @pl.when(there)
            def _():
                for h in range(rows):
                    coarse_wait(2 * src + 1 - core, h)
                conv_pair(src)

        @pl.when(jnp.logical_and(k > 1, k < chips - 1))
        def _():
            spread(k - 1)

        return carry

    lax.fori_loop(1, chips, step, 0)

    height = devices * rows
    for copy in small:
        copy.wait()
    values = summed[1 : height + 1].reshape(height * width, outputs) + conv_bias[...]
    scale = 1.0 / (height * width * GSIZE)
    same = (
        lax.broadcasted_iota(jnp.int32, (outputs, outputs), 0) // GSIZE
        == lax.broadcasted_iota(jnp.int32, (outputs, outputs), 1) // GSIZE
    ).astype(jnp.float32)

    def group_mean(array):
        each = jnp.broadcast_to(jnp.sum(array, axis=0, keepdims=True), (8, outputs))
        whole = jnp.dot(each, same, preferred_element_type=jnp.float32, precision=lax.Precision.HIGHEST)
        return whole[:1] * scale

    values = values - group_mean(values)
    factor = lax.rsqrt(group_mean(values * values) + 1e-05) * gain[...]
    normed = values * factor + shift[...]
    act[...] = (normed / (1.0 + jnp.exp(-normed))).astype(jnp.bfloat16).reshape(devices, rows * width, outputs)

    def act_copy(other, slot):
        return remote(act.at[other], act_all.at[slot], a_send.at[other], a_recv.at[slot], at(col, other))

    def send_act(i, carry):
        act_copy(lax.rem(me + i, devices), me).start()
        return carry

    lax.fori_loop(1, devices, send_act, 0)
    act_all[me] = act[me]

    if chips > 2:
        spread(chips - 2)

    def early(i, carry):
        other = lax.rem(me + i, devices)
        bias_copy(other, other).wait()
        return carry

    lax.fori_loop(1, devices, early, 0)

    def coarse_sent(src, carry):
        for h in range(rows):
            coarse_sib(src, h, gathered.at[0, h]).wait_send()
        for direction in range(2):
            passed = src <= z if direction == 0 else src >= z

            @pl.when(jnp.logical_and(passed, onward(direction)[1]))
            def _():
                for h in range(rows):
                    coarse_line(direction, src, h, gathered.at[0, h]).wait_send()
                up_line(direction, src, up_all.at[0, 0]).wait_send()

        return carry

    lax.fori_loop(0, chips, coarse_sent, 0)
    spread(chips - 1)
    for copy in up_copies:
        copy.wait()

    def arrivals(i, carry):
        other = lax.rem(me + i, devices)
        act_copy(other, other).wait()
        return carry

    lax.fori_loop(1, devices, arrivals, 0)

    def up_arrivals(src, carry):
        @pl.when(src != z)
        def _():
            for q in range(1, TAPS):
                up_xy(q, src).wait_send()

        up_sib(src, up_all.at[:, 0]).wait_send()
        b = 2 * src + 1 - core
        remote(up_all.at[:, b], up_all.at[:, b], u_sib.at[src], u_whole.at[b], at(col, sibling)).wait_recv()
        return carry

    lax.fori_loop(0, chips, up_arrivals, 0)

    bias = jnp.sum(bias_all[...], axis=0)[:1]
    for tap in range(TAPS):
        weight = up_all[tap].reshape(decoded, channels)
        if outputs % 128 == 0:
            features = jnp.concatenate([act_all[s] for s in range(devices)], axis=1)
            fine = lax.dot_general(features, weight, NT, preferred_element_type=jnp.float32)
        else:
            fine = jnp.zeros((rows * width, decoded), jnp.float32)
            for s in range(devices):
                fine = fine + lax.dot_general(
                    act_all[s],
                    weight[:, s * outputs : (s + 1) * outputs],
                    NT,
                    preferred_element_type=jnp.float32,
                )
        a, b = tap // 2, tap % 2
        for i in range(rows):
            values = fine[i * width : (i + 1) * width] + bias
            for t in range(decoded // 128):
                mixed[t, 2 * i + a, pl.ds(b, width, stride=2), :] = values[:, 128 * t : 128 * (t + 1)]
    for t in range(decoded // 128):
        out[:, :, 128 * t : 128 * (t + 1)] = mixed[t].astype(jnp.bfloat16)


def body(chips, coarse, conv_weight, conv_bias, norm_gain, norm_shift, up_weight, up_bias):
    devices = 2 * chips
    rows, width, channels = coarse.shape
    outputs = conv_weight.shape[0]
    slice_out = up_weight.shape[0]
    decoded = devices * slice_out
    conv_w = jnp.transpose(conv_weight, (1, 2, 0, 3)).reshape(9 * outputs, channels)
    up_w = jnp.transpose(up_weight, (1, 2, 0, 3)).reshape(TAPS, slice_out, channels)
    hbm = pl.BlockSpec(memory_space=pltpu.HBM)
    vmem = pl.BlockSpec(memory_space=pltpu.VMEM)
    dma = pltpu.SemaphoreType.DMA
    return pl.pallas_call(
        functools.partial(kernel, chips),
        out_shape=jax.ShapeDtypeStruct((2 * rows, 2 * width, decoded), jnp.bfloat16),
        in_specs=[hbm, hbm, pl.BlockSpec(memory_space=pl.ANY), hbm, hbm, hbm, hbm],
        out_specs=vmem,
        scratch_shapes=[
            pltpu.VMEM((devices, rows, width, channels), jnp.bfloat16),
            pltpu.VMEM((9 * outputs, channels), jnp.bfloat16),
            pltpu.VMEM((TAPS, devices, slice_out, channels), jnp.bfloat16),
            pltpu.VMEM((devices * rows + 2, width, outputs), jnp.float32),
            pltpu.VMEM((devices, rows * width, outputs), jnp.bfloat16),
            pltpu.VMEM((devices, rows * width, outputs), jnp.bfloat16),
            pltpu.VMEM((8, decoded), jnp.float32),
            pltpu.VMEM((devices, 8, decoded), jnp.float32),
            pltpu.VMEM((1, outputs), jnp.float32),
            pltpu.VMEM((1, outputs), jnp.float32),
            pltpu.VMEM((1, outputs), jnp.float32),
            pltpu.VMEM((decoded // 128, 2 * rows, 2 * width, 128), jnp.float32),
            pltpu.VMEM((slice_out,), jnp.bfloat16),
            dma((6 + TAPS,)),
            dma((2, chips, rows)),
            dma((chips, rows)),
            dma((devices, rows)),
            dma((2, chips)),
            dma((TAPS - 1, chips)),
            dma((chips,)),
            dma((devices, TAPS)),
            dma((devices,)),
            dma((devices,)),
            dma((devices,)),
            dma((devices,)),
            dma((devices,)),
        ],
        compiler_params=pltpu.CompilerParams(
            collective_id=0, has_side_effects=True, vmem_limit_bytes=60 * 1024 * 1024
        ),
    )(
        coarse,
        conv_w,
        up_w,
        conv_bias.reshape(1, outputs),
        norm_gain.reshape(1, outputs),
        norm_shift.reshape(1, outputs),
        up_bias,
    )


def solution(mesh):
    return jax.shard_map(
        functools.partial(body, mesh.shape["sp"] // 2),
        mesh=mesh,
        in_specs=(
            P(("grp", "sp"), None, None),
            P("sp", None, None, None),
            P("sp"),
            P("sp"),
            P("sp"),
            P("sp", None, None, None),
            P("sp"),
        ),
        out_specs=P(("grp", "sp"), None, None),
        check_vma=False,
    )
```
